128 devices in a mesh: region: 8 (over y, x_lo), shard: 16 (over x_hi, z, core).
Axes of the slice: x: 4 (x_hi: 2, x_lo: 2; x = x_hi * 2 + x_lo), y: 4, z: 4, core: 2. Of those that a mesh axis runs over, the one named last changes fastest.
Arguments:
- object_slices: float32 [3, 2, 8192, 512], P(None, None, ('region', 'shard')), may hold values from -4 to 4
- probe_field: float32 [2, 256, 256], replicated, may hold values from -4 to 4
- positions: int32 [128, 4, 2], P(('region', 'shard')), may hold values from 0 to 7936, as said below
- scan_counts: int32 [128], P(('region', 'shard')), may hold values from 1 to 4, 288 in all
- measured: float32 [128, 4, 256, 256], P(('region', 'shard')), may hold values from 0 to 2
Outputs:
- object_gradient: float32 [3, 2, 8192, 512], P(None, None, ('region', 'shard'))
- probe_gradient: float32 [2, 256, 256], replicated
The draws below stay inside these ranges and needn't reach their ends.
Inputs may be any that keep to these rules, and one draw needn't show every extreme that they name: `positions`: entry [d, j] is scan j of the device with linear index d over region, then shard. The scans of a device in region g start at rows g * 1024 to (g + 1) * 1024 - 256 and columns 0 to 256, so every window lies in that region's band of rows. Only the first scan_counts[d] scans of device d are measured and used.
All inputs are finite; a program needn't handle non-finite values.
Results may differ from the reference program's by a relative error of at most 0.0003.
Values sent between devices are 32-bit elements; how exact they have to be, the bound alone decides.
A program may use at most 192 MiB of HBM per device.

```python
import math
import jax
import jax.numpy as jnp
import numpy as np
from jax import lax

P_SIZE = 256
LAYERS = 3
TY = 64
NX = 512
SCANS = 4
NY = 8192
N_REGION = 8
N_SHARD = 16


def draw_positions(key, part):
    key = jax.random.fold_in(key, 7)
    row_key, column_key = jax.random.split(key)
    devices = N_REGION * N_SHARD
    band_rows = TY * N_SHARD
    row_offsets = jax.random.randint(row_key, (devices, SCANS), 0, band_rows - P_SIZE + 1)
    column_offsets = jax.random.randint(column_key, (devices, SCANS), 0, NX - P_SIZE + 1)
    row_offsets = row_offsets.at[0, 0].set(0)
    row_offsets = row_offsets.at[devices - 1, 0].set(band_rows - P_SIZE)
    column_offsets = column_offsets.at[0, 0].set(0)
    column_offsets = column_offsets.at[devices - 1, 0].set(NX - P_SIZE)
    region_index = jnp.arange(devices, dtype=jnp.int32) // N_SHARD
    row_offsets = row_offsets + (region_index * band_rows)[:, None]
    return jnp.stack([row_offsets, column_offsets], -1).astype(jnp.int32)


def levels(own_key, extent, shards, smallest, largest):
    def one(position, blocks):
        draws = jax.random.uniform(jax.random.fold_in(jax.random.fold_in(own_key, 6), position), (blocks,), jnp.float32, smallest / len(shards), largest / len(shards))
        return jnp.repeat(jnp.exp(draws), extent[position] // blocks).reshape((-1,) + (1,) * (len(extent) - position - 1))

    loudness = one(*shards[0])
    for cut in shards[1:]:
        loudness = loudness * one(*cut)
    return loudness


def length_profile(count, total, reach, skew):
    loads = [(1 << 20) // math.isqrt(standing ** skew) + 1 for standing in range(2, count + 1)]
    spare, holding = total - reach - (count - 1), [1] * (count - 1)
    while spare > 0:
        movable = [i for i in range(count - 1) if holding[i] < reach]
        mass, remaining = sum([loads[i] for i in movable]), spare
        for i in movable:
            addition = min(reach - holding[i], max(1, remaining * loads[i] // mass), spare)
            holding[i] = holding[i] + addition
            spare = spare - addition
    return np.array([reach] + holding)


def uneven_parts(own_key, count, total, most, skew):
    if count == 2:
        one = jax.random.randint(own_key, (), max(1, total - most), min(most, total - 1) + 1)
        return jnp.stack([one, total - one])
    sizes = jnp.asarray(length_profile(count, total, most, skew), jnp.int32)
    couples = (count - 1) // 2
    source_of, sink = sizes[1:1 + 2 * couples:2], sizes[2:2 + 2 * couples:2]
    room = jnp.minimum(source_of - 1, most - sink)
    moved = jax.random.randint(jax.random.fold_in(own_key, 1), (couples,), 0, 1 << 20) % (room + 1)
    sizes = sizes.at[1:1 + 2 * couples:2].set(source_of - moved).at[2:2 + 2 * couples:2].set(sink + moved)
    return sizes[jax.random.permutation(jax.random.fold_in(own_key, 2), count)]


def normal_values(own_key, extent, scale, reach, cuts=(), kind=jnp.bfloat16):
    loudness = levels(own_key, extent, cuts, -0.22, 0.18) if cuts else 1.0
    drawn = jax.random.normal(own_key, extent, jnp.float32) * scale * loudness
    return jnp.minimum(jnp.maximum(drawn, -reach), reach).astype(kind)


def setup_inputs(seed: int = 0) -> dict:
    streams_of = jax.random.split(jax.random.key(seed), 6)
    return {
        "object_slices": normal_values(streams_of[0], (LAYERS, 2, NY, NX), 0.7, 4.0, ((2, 128),), jnp.float32),
        "probe_field": normal_values(streams_of[1], (2, P_SIZE, P_SIZE), 0.7, 4.0, (), jnp.float32),
        "positions": draw_positions(jax.random.fold_in(streams_of[5], 71), 0),
        "scan_counts": uneven_parts(streams_of[3], N_REGION * N_SHARD, N_REGION * N_SHARD * (2 * SCANS + 1) // 4, SCANS, 2).astype(jnp.int32),
        "measured": jnp.clip(2.0 * jax.random.uniform(streams_of[4], (N_REGION * N_SHARD, SCANS, P_SIZE, P_SIZE), jnp.float32) ** levels(streams_of[4], (N_REGION * N_SHARD, SCANS, P_SIZE, P_SIZE), ((0, 128),), -0.2, 0.2), 0.0, 2.0),
    }


phase_rate = 20.0


def frequency_tables(length):
    indices = jnp.arange(length, dtype=jnp.int32)
    signed_freq = ((indices + length // 2) % length) - length // 2
    scaled = signed_freq.astype(jnp.float32) / length
    squared = scaled[:, None] * scaled[:, None] + scaled[None, :] * scaled[None, :]
    inside = (signed_freq[:, None] * signed_freq[:, None] + signed_freq[None, :] * signed_freq[None, :] <= (length // 3) ** 2).astype(jnp.float32)
    phase_angle = phase_rate * squared
    return inside * jnp.cos(phase_angle), -inside * jnp.sin(phase_angle)


def forward_two(field):
    return jnp.fft.fft2(field, norm="ortho")


def inverse_two(field):
    return jnp.fft.ifft2(field, norm="ortho")


def reference(object_slices, probe_field, positions, scan_counts, measured):
    kernel_real, kernel_imag = frequency_tables(P_SIZE)
    propagator = kernel_real + 1j * kernel_imag
    probe_wave = probe_field[0] + 1j * probe_field[1]
    devices = N_REGION * N_SHARD
    alive_mask = (jnp.arange(SCANS, dtype=jnp.int32)[None, :] < scan_counts[:, None]).astype(jnp.float32)
    flat_positions = positions.reshape(devices * SCANS, 2).astype(jnp.int32)
    flat_measured = measured.reshape(devices * SCANS, P_SIZE, P_SIZE)
    flat_alive = alive_mask.reshape(devices * SCANS)
    zero_index = jnp.zeros((), jnp.int32)

    def single_scan(state_carry, inputs):
        gradient, probe_sum = state_carry
        offsets, target, alive = inputs
        corner = (zero_index, zero_index, offsets[0].astype(jnp.int32), offsets[1].astype(jnp.int32))
        patch = lax.dynamic_slice(object_slices, corner, (LAYERS, 2, P_SIZE, P_SIZE))
        transmit = patch[:, 0] + 1j * patch[:, 1]
        fields = []
        wave = probe_wave
        for layer_index in range(LAYERS):
            fields.append(wave)
            wave = wave * transmit[layer_index]
            if layer_index + 1 < LAYERS:
                wave = inverse_two(forward_two(wave) * propagator)
        far_field = forward_two(wave)
        intensity = jnp.real(far_field) * jnp.real(far_field) + jnp.imag(far_field) * jnp.imag(far_field)
        residual = (intensity - target) * alive
        adjoint = inverse_two(residual * far_field)
        pieces = [None] * LAYERS
        for layer_index in reversed(range(LAYERS)):
            piece = jnp.conj(fields[layer_index]) * adjoint
            pieces[layer_index] = jnp.stack([jnp.real(piece), jnp.imag(piece)])
            adjoint = jnp.conj(transmit[layer_index]) * adjoint
            if layer_index > 0:
                adjoint = inverse_two(forward_two(adjoint) * jnp.conj(propagator))
        update = jnp.stack(pieces)
        current = lax.dynamic_slice(gradient, corner, (LAYERS, 2, P_SIZE, P_SIZE))
        gradient = lax.dynamic_update_slice(gradient, current + update, corner)
        probe_sum = probe_sum + jnp.stack([jnp.real(adjoint), jnp.imag(adjoint)])
        return (gradient, probe_sum), None

    start_gradient = jnp.zeros(object_slices.shape, jnp.float32)
    start_probe = jnp.zeros((2, P_SIZE, P_SIZE), jnp.float32)
    (gradient, probe_sum), _ = lax.scan(single_scan, (start_gradient, start_probe), (flat_positions, flat_measured, flat_alive))
    scale_factor = (N_REGION * N_SHARD) ** -0.5
    return gradient, probe_sum * scale_factor
```

```python
import functools

import jax
import jax.numpy as jnp
import numpy as np
from jax import lax
from jax.experimental import pallas as pl
from jax.experimental.pallas import tpu as pltpu
from jax.sharding import PartitionSpec as P

MESH = pl.DeviceIdType.MESH
bf16, f32 = jnp.bfloat16, jnp.float32
cat = jnp.concatenate
SIDE, HALF = 256, 128
LAYERS, SCANS = 3, 4
ROWS, COLS, BAND = 64, 512, 1024
REGIONS, SHARDS, CHIPS = 8, 16, 8
PROBE_ROWS = SIDE // SHARDS


def transform_tables():
    index = np.arange(HALF)
    found = []
    for parity in (0, 1):
        angle = 2 * np.pi * ((index[:, None] * (2 * index + parity)[None, :]) % SIDE) / SIDE
        c, s = np.cos(angle) / np.sqrt(SIDE), np.sin(angle) / np.sqrt(SIDE)
        whole = np.block([[c, -s], [s, c]]).astype(np.float32)
        high = whole.astype(bf16)
        found += [high, (whole - high.astype(np.float32)).astype(bf16)]
    table = np.stack(found)
    return table, np.ascontiguousarray(table.transpose(0, 2, 1))


def order():
    return np.concatenate([np.arange(0, SIDE, 2), np.arange(1, SIDE, 2)])


def propagator():
    signed = ((np.arange(SIDE) + HALF) % SIDE - HALF)[order()]
    scaled = signed.astype(np.float32) / np.float32(SIDE)
    squared = scaled[:, None] * scaled[:, None] + scaled[None, :] * scaled[None, :]
    inside = (signed[:, None] ** 2 + signed[None, :] ** 2 <= (SIDE // 3) ** 2).astype(np.float64)
    angle = (np.float32(20.0) * squared).astype(np.float64)
    return np.stack([inside * np.cos(angle), -inside * np.sin(angle)]).astype(np.float32)


def shuffles():
    even_first = np.zeros((SIDE, SIDE), np.float32)
    even_first[order(), np.arange(SIDE)] = 1
    return np.stack([even_first, even_first.T]).astype(bf16)


def split(x):
    high = x.astype(bf16)
    return high, (x - high.astype(f32)).astype(bf16)


def dot(a, b):
    return jnp.dot(a, b, preferred_element_type=f32)


def times_table(x, table, which):
    high, low = split(x)
    return dot(high, table[2 * which]) + dot(low, table[2 * which]) + dot(high, table[2 * which + 1])


def table_times(table, which, x):
    high, low = split(x)
    return dot(table[2 * which], high) + dot(table[2 * which], low) + dot(table[2 * which + 1], high)


def forward(re, im, tab, tab_t):
    h = HALF
    even = times_table(cat([re[:, :h] + re[:, h:], im[:, :h] + im[:, h:]], 1), tab, 0)
    odd = times_table(cat([re[:, :h] - re[:, h:], im[:, :h] - im[:, h:]], 1), tab, 1)
    se, so, de, do = even[:h] + even[h:], odd[:h] + odd[h:], even[:h] - even[h:], odd[:h] - odd[h:]
    top = cat([cat([se[:, :h], so[:, :h]], 1), cat([se[:, h:], so[:, h:]], 1)], 0)
    low = cat([cat([de[:, :h], do[:, :h]], 1), cat([de[:, h:], do[:, h:]], 1)], 0)
    return table_times(tab_t, 0, top), table_times(tab_t, 1, low)


def inverse(even, odd, tab, tab_t):
    h = HALF
    a, b = table_times(tab, 0, even), table_times(tab, 1, odd)
    top, low = a + b, a - b
    e = cat([cat([top[:h, :h], top[h:, :h]], 1), cat([low[:h, :h], low[h:, :h]], 1)], 0)
    o = cat([cat([top[:h, h:], top[h:, h:]], 1), cat([low[:h, h:], low[h:, h:]], 1)], 0)
    a, b = times_table(e, tab_t, 0), times_table(o, tab_t, 1)
    left, right = a + b, a - b
    return cat([left[:, :h], right[:, :h]], 1), cat([left[:, h:], right[:, h:]], 1)


def multiply(ar, ai, br, bi):
    return ar * br - ai * bi, ar * bi + ai * br


def conj_multiply(ar, ai, br, bi):
    return ar * br + ai * bi, ar * bi - ai * br


def propagate(re, im, tab, tab_t, kern, adjoint):
    parts = []
    for at, y in zip((0, HALF), forward(re, im, tab, tab_t)):
        hr, hi = kern[0, at : at + HALF, :], kern[1, at : at + HALF, :]
        parts.append(cat((conj_multiply if adjoint else multiply)(hr, hi, y[:HALF], y[HALF:]), 0))
    return inverse(*parts, tab, tab_t)


class Place:
    def __init__(self):
        self.region, self.shard = lax.axis_index("region"), lax.axis_index("shard")
        self.core = lax.rem(self.shard, 2)
        self.chip = self.shard // 2
        self.z, self.side = lax.rem(self.chip, 4), self.chip // 4
        self.up, self.down, self.far = [lax.rem(self.z + d, 4) for d in (1, 3, 2)]
        self.sibling = self.device(self.chip, 1 - self.core)
        self.across = self.device(self.at(1 - self.side, self.z))
        self.above = self.device(self.at(self.side, self.up))
        self.below = self.device(self.at(self.side, self.down))

    def at(self, side, z):
        return side * 4 + z

    def device(self, chip, core=None):
        return (self.region, chip * 2 + (self.core if core is None else core))

    def greet(self, devices):
        barrier = pltpu.get_barrier_semaphore()
        for device in devices:
            pl.semaphore_signal(barrier, inc=1, device_id=device, device_id_type=MESH)
        pl.semaphore_wait(barrier, len(devices))


class Links:
    def __init__(self, send, recv):
        self.send, self.recv, self.count, self.names = send, recv, 0, {}

    def go(self, name, source, target, device):
        n, self.count = self.count, self.count + 1
        copy = pltpu.make_async_remote_copy(
            src_ref=source, dst_ref=target, send_sem=self.send.at[n], recv_sem=self.recv.at[n],
            device_id=device, device_id_type=MESH,
        )
        copy.start()
        self.names[name] = copy

    def got(self, name):
        self.names[name].wait_recv()

    def settle(self, chosen=lambda name: True):
        for name in [name for name in self.names if chosen(name)]:
            self.names.pop(name).wait_send()


def gather_round(step, layer, links, place, own, panel):
    p_, half = place, ROWS // 2
    here, there = p_.side, 1 - p_.side

    def rows(side, z, part, cut=None):
        start = p_.device(p_.at(side, z))[1] * ROWS
        if cut is None:
            return panel.at[part, pl.ds(pl.multiple_of(start, ROWS), ROWS), :]
        return panel.at[part, pl.ds(pl.multiple_of(start + cut * half, half), half), :]

    def go(name, part, piece, device, source=None):
        links.go((layer, part, name), piece if source is None else source, piece, device)

    def got(name, part, piece):
        links.got((layer, part, name))
        go("s" + name, part, piece, p_.sibling)

    if step == 0:
        for part in (0, 1):
            mine, source = rows(here, p_.z, part), own.at[layer, part]
            go("m", part, mine, p_.above, source)
            go("p", part, mine, p_.below, source)
            go("x", part, mine, p_.across, source)
            go("s", part, mine, p_.sibling, source)
    if step == 1:
        for name, z, ahead, cut in (("m", p_.down, p_.above, 0), ("p", p_.up, p_.below, 1)):
            for part in (0, 1):
                got(name, part, rows(here, z, part))
                go("h" + name, part, rows(here, z, part, cut), ahead)
            go("x" + name, 1, rows(here, z, 1), p_.across)
        for part in (0, 1):
            got("x", part, rows(there, p_.z, part))
        go("xm", 0, rows(there, p_.z, 0), p_.above)
        go("xp", 0, rows(there, p_.z, 0), p_.below)
    if step == 2:
        for name, cut in (("hm", 0), ("hp", 1)):
            for part in (0, 1):
                got(name, part, rows(here, p_.far, part, cut))
            go("x" + name, 1, rows(here, p_.far, 1, cut), p_.across)
        for name, z, ahead, cut in (("m", p_.down, p_.above, 0), ("p", p_.up, p_.below, 1)):
            for part in (0, 1):
                got("x" + name, part, rows(there, z, part))
            go("xh" + name, 0, rows(there, z, 0, cut), ahead)
    if step == 3:
        for name, cut in (("xhm", 0), ("xhp", 1)):
            for part in (0, 1):
                got(name, part, rows(there, p_.far, part, cut))
    if step == 4:
        for part in (0, 1):
            for name in ("", "m", "p", "x", "hm", "hp", "xm", "xp", "xhm", "xhp"):
                links.got((layer, part, "s" + name))


GATHER_COPIES = 2 * 4 + 2 * 9 + 4 + 2 + 2 + 2 + 2


def sum_round(step, layer, links, place, band, bufs, out):
    p_, half = place, ROWS // 2
    here, there = p_.side, 1 - p_.side
    acc, halves, fulls, cross, halves_b, fulls_b, cross_b = bufs
    top, low = pl.ds(0, half), pl.ds(half, half)

    def go(name, source, target, device):
        links.go(("sum", layer, name), source, target, device)

    def got(name):
        links.got(("sum", layer, name))

    def rows(chip, core):
        return pl.ds(pl.multiple_of((chip * 2 + core) * ROWS, ROWS), ROWS)

    if step == 0:
        for chip in range(CHIPS):
            go(("s", chip), band.at[:, rows(chip, 1 - p_.core), :], acc.at[chip], p_.sibling)
    if step == 1:
        for chip in range(CHIPS):
            got(("s", chip))
            acc[chip] = acc[chip] + band[:, rows(chip, p_.core), :]
        for n, side in enumerate((here, there)):
            far = p_.at(side, p_.far)
            go(("h", 0, n), acc.at[far, 0, top], halves.at[0, n], p_.above)
            go(("h", 1, n), acc.at[far, 0, low], halves.at[1, n], p_.below)
        for z in range(4):
            go(("x", z), acc.at[p_.at(there, z), 1], cross_b.at[z], p_.across)
    if step == 2:
        for n, side in enumerate((here, there)):
            for way, z, cut, ahead in ((0, p_.up, top, p_.above), (1, p_.down, low, p_.below)):
                got(("h", way, n))
                chip = p_.at(side, z)
                acc[chip, 0, cut] = acc[chip, 0, cut] + halves[way, n]
                go(("f", way, n), acc.at[chip, 0], fulls.at[way, n], ahead)
        for z in range(4):
            got(("x", z))
            chip = p_.at(here, z)
            acc[chip, 1] = acc[chip, 1] + cross_b[z]
        far = p_.at(here, p_.far)
        go(("hb", 0), acc.at[far, 1, top], halves_b.at[0], p_.above)
        go(("hb", 1), acc.at[far, 1, low], halves_b.at[1], p_.below)
    if step == 3:
        for n, side in reversed(list(enumerate((here, there)))):
            chip = p_.at(side, p_.z)
            for way in (0, 1):
                got(("f", way, n))
            acc[chip, 0] = acc[chip, 0] + fulls[0, n] + fulls[1, n]
            if n == 1:
                go("c", acc.at[chip, 0], cross, p_.across)
        for way, z, cut, ahead in ((0, p_.up, top, p_.above), (1, p_.down, low, p_.below)):
            got(("hb", way))
            chip = p_.at(here, z)
            acc[chip, 1, cut] = acc[chip, 1, cut] + halves_b[way]
            go(("fb", way), acc.at[chip, 1], fulls_b.at[way], ahead)
    if step == 4:
        mine = p_.at(here, p_.z)
        for way in (0, 1):
            got(("fb", way))
        out[layer, 1] = acc[mine, 1] + fulls_b[0] + fulls_b[1]
        got("c")
        out[layer, 0] = acc[mine, 0] + cross[...]


SUM_COPIES = 8 + 4 + 4 + 4 + 2 + 1 + 2
SUM_BUFFERS = [
    pltpu.VMEM((CHIPS, 2, ROWS, COLS), f32),
    pltpu.VMEM((2, 2, ROWS // 2, COLS), f32),
    pltpu.VMEM((2, 2, ROWS, COLS), f32),
    pltpu.VMEM((ROWS, COLS), f32),
    pltpu.VMEM((2, ROWS // 2, COLS), f32),
    pltpu.VMEM((2, ROWS, COLS), f32),
    pltpu.VMEM((4, ROWS, COLS), f32),
]


def probe_round(step, links, place, part, bufs, out):
    p_ = place
    acc, mine, all_regions = bufs

    def go(name, source, target, device):
        links.go(("probe", name), source, target, device)

    def got(name):
        links.got(("probe", name))

    def rows(shard):
        return pl.ds(pl.multiple_of(shard * PROBE_ROWS, PROBE_ROWS), PROBE_ROWS)

    if step == 0:
        for chip in range(CHIPS):
            go(("s", chip), part.at[:, rows(chip * 2 + 1 - p_.core), :], acc.at[chip], p_.sibling)
    if step == 1:
        for chip in range(CHIPS):
            got(("s", chip))
            acc[chip] = acc[chip] + part[:, rows(chip * 2 + p_.core), :]
        for d in range(1, CHIPS):
            chip = lax.rem(p_.chip + d, CHIPS)
            go(("r", d), acc.at[chip], mine.at[d], p_.device(chip))
    if step == 2:
        total = acc[p_.chip]
        for d in range(1, CHIPS):
            got(("r", d))
            total = total + mine[d]
        all_regions[p_.region] = total
        for d in range(1, REGIONS):
            go(("g", d), all_regions.at[p_.region], all_regions.at[p_.region], (lax.rem(p_.region + d, REGIONS), p_.shard))
    if step == 3:
        for d in range(1, REGIONS):
            got(("g", d))
        total = all_regions[0]
        for region in range(1, REGIONS):
            total = total + all_regions[region]
        out[:, rows(p_.shard), :] = total * (REGIONS * SHARDS) ** -0.5
        for d in range(1, SHARDS):
            there = lax.rem(p_.shard + d, SHARDS)
            go(("b", d), out.at[:, rows(p_.shard), :], out.at[:, rows(p_.shard), :], (p_.region, there))
    if step == 4:
        for d in range(1, SHARDS):
            got(("b", d))


PROBE_COPIES = 8 + 7 + 7 + 15
PROBE_BUFFERS = [
    pltpu.VMEM((CHIPS, 2, PROBE_ROWS, SIDE), f32),
    pltpu.VMEM((CHIPS, 2, PROBE_ROWS, SIDE), f32),
    pltpu.VMEM((REGIONS, 2, PROBE_ROWS, SIDE), f32),
]


def probe_partners(place):
    chips = [place.device(lax.rem(place.chip + d, CHIPS)) for d in range(1, CHIPS)]
    regions = [(lax.rem(place.region + d, REGIONS), place.shard) for d in range(1, REGIONS)]
    return chips, regions


def kernel(corners, alive, own, probe, measured, tab, tab_t, kern, mix, out, probe_out, *scratch):
    panels, scratch = scratch[:LAYERS], scratch[LAYERS:]
    sums, scratch = [scratch[7 * n : 7 * n + 7] for n in range(LAYERS)], scratch[7 * LAYERS :]
    probe_bufs, scratch = scratch[:3], scratch[3:]
    window, psi, chi, target, placed, probe_sum, send_sem, recv_sem = scratch
    place = Place()
    links = Links(send_sem, recv_sem)
    chips, regions = probe_partners(place)
    place.greet([place.sibling] + chips + regions + [place.device(lax.rem(place.chip + d, CHIPS), 1 - place.core) for d in range(1, CHIPS)])

    def gather(layer, step):
        gather_round(step, layer, links, place, own, panels[layer])

    def collect(layer, step):
        sum_round(step, layer, links, place, panels[layer], sums[layer], out)

    def collect_probe(step):
        probe_round(step, links, place, probe_sum, probe_bufs, probe_out)

    def scans(first, last, body):
        def step(scan, carry):
            body(scan)
            return carry

        lax.fori_loop(first, last, step, 0)

    def fetch(scan, layer):
        row, column = corners[0, scan], corners[1, scan]
        index = lax.broadcasted_iota(jnp.int32, (SIDE, SIDE), 0)
        in_left = lax.broadcasted_iota(jnp.int32, (SIDE, SIDE), 1) >= column
        for part in (0, 1):
            found = None
            for first in range(BAND - SIDE, -1, -SIDE):
                rows = slice(first, first + SIDE)
                piece = jnp.where(in_left, panels[layer][part, rows, :SIDE], panels[layer][part, rows, SIDE:])
                found = piece if found is None else jnp.where(index >= row - first, piece, found)
            window[scan, layer, part] = found

    def turned(x, scan, back):
        row, column = corners[0, scan], corners[1, scan]
        a = lax.broadcasted_iota(jnp.int32, (SIDE, SIDE), 0)
        b = lax.broadcasted_iota(jnp.int32, (SIDE, SIDE), 1)
        down, along = (b - a - row, a - b - column) if back else (a - b - row, b - a - column)
        down, along = [
            jnp.where(jnp.bitwise_and(far, SIDE - 1) == 0, 1.0, 0.0).astype(bf16) for far in (down, along)
        ]
        high, low = split(x)
        high, low = split(dot(high, along) + dot(low, along))
        return dot(down, high) + dot(down, low)

    def assemble(layer, core):
        def one(chip, carry):
            first = (chip * 2 + core) * ROWS
            source = pl.ds(pl.multiple_of(lax.rem(first, SIDE), ROWS), ROWS)
            target = pl.ds(pl.multiple_of(first, ROWS), ROWS)
            rows = lax.broadcasted_iota(jnp.int32, (ROWS, SIDE), 0) + first
            columns = lax.broadcasted_iota(jnp.int32, (ROWS, SIDE), 1)
            total = [[None, None], [None, None]]
            for scan in range(SCANS):
                row, column = corners[0, scan], corners[1, scan]
                inside = jnp.logical_and(rows >= row, rows < row + SIDE)
                left = jnp.logical_and(inside, columns >= column)
                right = jnp.logical_and(inside, columns < column)
                for part in (0, 1):
                    piece = placed[scan, part, source, :]
                    for n, mask in enumerate((left, right)):
                        add = jnp.where(mask, piece, 0.0)
                        total[part][n] = add if scan == 0 else total[part][n] + add
            for part in (0, 1):
                for n in (0, 1):
                    panels[layer][part, target, n * SIDE : (n + 1) * SIDE] = total[part][n]
            return carry

        lax.fori_loop(0, CHIPS, one, 0)

    def reorder(scan):
        rows = None
        for piece in split(measured[0, scan]):
            rows = dot(piece, mix[0]) + (0 if rows is None else rows)
        both = None
        for piece in split(rows):
            both = dot(mix[1], piece) + (0 if both is None else both)
        target[scan] = both

    def illuminate(scan):
        for part in (0, 1):
            psi[scan, 0, part] = turned(probe[part], scan, False)

    def wave(scan, layer):
        return psi[scan, layer, 0], psi[scan, layer, 1]

    def enter(scan, layer):
        fetch(scan, layer)
        return multiply(*wave(scan, layer), window[scan, layer, 0], window[scan, layer, 1])

    def go_on(layer):
        def body(scan):
            re, im = propagate(*enter(scan, layer), tab, tab_t, kern, False)
            psi[scan, layer + 1, 0], psi[scan, layer + 1, 1] = re, im

        return body

    def leave(scan, layer, re, im):
        placed[scan, 0], placed[scan, 1] = conj_multiply(*wave(scan, layer), re, im)
        re, im = conj_multiply(window[scan, layer, 0], window[scan, layer, 1], re, im)
        if layer > 0:
            chi[scan, 0], chi[scan, 1] = re, im
        else:
            probe_sum[0] = probe_sum[0] + turned(re, scan, True)
            probe_sum[1] = probe_sum[1] + turned(im, scan, True)

    def turn(scan):
        parts = []
        for at, y in zip((0, HALF), forward(*enter(scan, LAYERS - 1), tab, tab_t)):
            re, im = y[:HALF], y[HALF:]
            residual = (re * re + im * im - target[scan, at : at + HALF, :]) * alive[scan]
            parts.append(cat([residual * re, residual * im], 0))
        leave(scan, LAYERS - 1, *inverse(*parts, tab, tab_t))

    def go_back(layer):
        def body(scan):
            leave(scan, layer, *propagate(chi[scan, 0], chi[scan, 1], tab, tab_t, kern, True))

        return body

    def give(layer):
        links.settle(lambda name: name[0] == layer)
        assemble(layer, 1 - place.core)
        collect(layer, 0)
        assemble(layer, place.core)

    gather(0, 0)
    for layer in range(LAYERS):
        for part in (0, 1):
            panels[layer][part, pl.ds(pl.multiple_of(place.shard * ROWS, ROWS), ROWS), :] = own[layer, part]
    probe_sum[...] = jnp.zeros_like(probe_sum)
    gather(0, 1)
    gather(1, 0)
    gather(0, 2)
    gather(1, 1)
    gather(2, 0)
    scans(0, SCANS, reorder)
    scans(0, SCANS, illuminate)
    gather(0, 3)
    gather(1, 2)
    gather(2, 1)
    gather(0, 4)
    scans(0, 2, go_on(0))
    gather(1, 3)
    gather(2, 2)
    scans(2, 4, go_on(0))
    gather(1, 4)
    gather(2, 3)
    scans(0, 4, go_on(1))
    gather(2, 4)
    scans(0, 4, turn)
    give(2)
    collect(2, 1)
    scans(0, 2, go_back(1))
    collect(2, 2)
    scans(2, 4, go_back(1))
    collect(2, 3)
    give(1)
    collect(1, 1)
    scans(0, 2, go_back(0))
    collect(2, 4)
    collect(1, 2)
    scans(2, 4, go_back(0))
    collect_probe(0)
    collect(1, 3)
    give(0)
    collect(0, 1)
    collect_probe(1)
    collect(1, 4)
    collect(0, 2)
    collect_probe(2)
    collect(0, 3)
    collect_probe(3)
    collect(0, 4)
    collect_probe(4)
    links.settle()


def body(object_slices, probe_field, positions, scan_counts, measured):
    band_start = lax.axis_index("region") * BAND
    row = jnp.clip(positions[0, :, 0] - band_start, 0, BAND - SIDE)
    column = jnp.clip(positions[0, :, 1], 0, COLS - SIDE)
    corners = jnp.stack([row, column])
    alive = (jnp.arange(SCANS, dtype=jnp.int32) < scan_counts[0]).astype(f32)
    tab, tab_t = transform_tables()
    vmem, smem = pl.BlockSpec(memory_space=pltpu.VMEM), pl.BlockSpec(memory_space=pltpu.SMEM)
    copies = LAYERS * (GATHER_COPIES + SUM_COPIES) + PROBE_COPIES
    field = (SIDE, SIDE)
    return pl.pallas_call(
        kernel,
        out_shape=(
            jax.ShapeDtypeStruct((LAYERS, 2, ROWS, COLS), f32),
            jax.ShapeDtypeStruct((2, *field), f32),
        ),
        in_specs=[smem, smem] + [vmem] * 7,
        out_specs=(vmem, vmem),
        scratch_shapes=[pltpu.VMEM((2, BAND, COLS), f32)] * LAYERS
        + SUM_BUFFERS * LAYERS
        + PROBE_BUFFERS
        + [
            pltpu.VMEM((SCANS, LAYERS, 2, *field), f32),
            pltpu.VMEM((SCANS, LAYERS, 2, *field), f32),
            pltpu.VMEM((SCANS, 2, *field), f32),
            pltpu.VMEM((SCANS, *field), f32),
            pltpu.VMEM((SCANS, 2, *field), f32),
            pltpu.VMEM((2, *field), f32),
            pltpu.SemaphoreType.DMA((copies,)),
            pltpu.SemaphoreType.DMA((copies,)),
        ],
        compiler_params=pltpu.CompilerParams(collective_id=0, has_side_effects=True, vmem_limit_bytes=60 * 2**20),
    )(corners, alive, object_slices, probe_field, measured, tab, tab_t, propagator(), shuffles())


def solution(mesh):
    return jax.shard_map(
        body,
        mesh=mesh,
        in_specs=(
            P(None, None, ("region", "shard"), None),
            P(),
            P(("region", "shard"), None, None),
            P(("region", "shard")),
            P(("region", "shard"), None, None, None),
        ),
        out_specs=(P(None, None, ("region", "shard"), None), P()),
        check_vma=False,
    )
```

```python
import functools

import jax
import jax.numpy as jnp
import numpy as np
from jax import lax
from jax.experimental import pallas as pl
from jax.experimental.pallas import tpu as pltpu
from jax.sharding import PartitionSpec as P

MESH = pl.DeviceIdType.MESH
bf16, f32 = jnp.bfloat16, jnp.float32
cat = jnp.concatenate
SIDE, HALF = 256, 128
LAYERS, SCANS = 3, 4
ROWS, COLS, BAND = 64, 512, 1024
REGIONS, SHARDS, CHIPS = 8, 16, 8
PROBE_ROWS = SIDE // SHARDS


def transform_tables():
    index = np.arange(HALF)
    found = []
    for parity in (0, 1):
        angle = 2 * np.pi * ((index[:, None] * (2 * index + parity)[None, :]) % SIDE) / SIDE
        c, s = np.cos(angle) / np.sqrt(SIDE), np.sin(angle) / np.sqrt(SIDE)
        whole = np.block([[c, -s], [s, c]]).astype(np.float32)
        high = whole.astype(bf16)
        found += [high, (whole - high.astype(np.float32)).astype(bf16)]
    table = np.stack(found)
    return table, np.ascontiguousarray(table.transpose(0, 2, 1))


def order():
    return np.concatenate([np.arange(0, SIDE, 2), np.arange(1, SIDE, 2)])


def propagator():
    signed = ((np.arange(SIDE) + HALF) % SIDE - HALF)[order()]
    scaled = signed.astype(np.float32) / np.float32(SIDE)
    squared = scaled[:, None] * scaled[:, None] + scaled[None, :] * scaled[None, :]
    inside = (signed[:, None] ** 2 + signed[None, :] ** 2 <= (SIDE // 3) ** 2).astype(np.float64)
    angle = (np.float32(20.0) * squared).astype(np.float64)
    return np.stack([inside * np.cos(angle), -inside * np.sin(angle)]).astype(np.float32)


def shuffles():
    even_first = np.zeros((SIDE, SIDE), np.float32)
    even_first[order(), np.arange(SIDE)] = 1
    return np.stack([even_first, even_first.T]).astype(bf16)


def split(x):
    high = x.astype(bf16)
    return high, (x - high.astype(f32)).astype(bf16)


def dot(a, b):
    return jnp.dot(a, b, preferred_element_type=f32)


def times_table(x, table, which):
    high, low = split(x)
    return dot(high, table[2 * which]) + dot(low, table[2 * which]) + dot(high, table[2 * which + 1])


def table_times(table, which, x):
    high, low = split(x)
    return dot(table[2 * which], high) + dot(table[2 * which], low) + dot(table[2 * which + 1], high)


def forward(re, im, tab, tab_t):
    h = HALF
    even = times_table(cat([re[:, :h] + re[:, h:], im[:, :h] + im[:, h:]], 1), tab, 0)
    odd = times_table(cat([re[:, :h] - re[:, h:], im[:, :h] - im[:, h:]], 1), tab, 1)
    se, so, de, do = even[:h] + even[h:], odd[:h] + odd[h:], even[:h] - even[h:], odd[:h] - odd[h:]
    top = cat([cat([se[:, :h], so[:, :h]], 1), cat([se[:, h:], so[:, h:]], 1)], 0)
    low = cat([cat([de[:, :h], do[:, :h]], 1), cat([de[:, h:], do[:, h:]], 1)], 0)
    return table_times(tab_t, 0, top), table_times(tab_t, 1, low)


def inverse(even, odd, tab, tab_t):
    h = HALF
    a, b = table_times(tab, 0, even), table_times(tab, 1, odd)
    top, low = a + b, a - b
    e = cat([cat([top[:h, :h], top[h:, :h]], 1), cat([low[:h, :h], low[h:, :h]], 1)], 0)
    o = cat([cat([top[:h, h:], top[h:, h:]], 1), cat([low[:h, h:], low[h:, h:]], 1)], 0)
    a, b = times_table(e, tab_t, 0), times_table(o, tab_t, 1)
    left, right = a + b, a - b
    return cat([left[:, :h], right[:, :h]], 1), cat([left[:, h:], right[:, h:]], 1)


def multiply(ar, ai, br, bi):
    return ar * br - ai * bi, ar * bi + ai * br


def conj_multiply(ar, ai, br, bi):
    return ar * br + ai * bi, ar * bi - ai * br


def propagate(re, im, tab, tab_t, kern, adjoint):
    parts = []
    for at, y in zip((0, HALF), forward(re, im, tab, tab_t)):
        hr, hi = kern[0, at : at + HALF, :], kern[1, at : at + HALF, :]
        parts.append(cat((conj_multiply if adjoint else multiply)(hr, hi, y[:HALF], y[HALF:]), 0))
    return inverse(*parts, tab, tab_t)


class Place:
    def __init__(self):
        self.region, self.shard = lax.axis_index("region"), lax.axis_index("shard")
        self.core = lax.rem(self.shard, 2)
        self.chip = self.shard // 2
        self.z, self.side = lax.rem(self.chip, 4), self.chip // 4
        self.other, self.rest = 1 - self.side, 1 - self.core
        self.up, self.down, self.far = [lax.rem(self.z + d, 4) for d in (1, 3, 2)]
        self.sibling = self.device(self.chip, 1 - self.core)
        self.across = self.device(self.at(1 - self.side, self.z))
        self.above = self.device(self.at(self.side, self.up))
        self.below = self.device(self.at(self.side, self.down))
        line, near = self.region // 2, lax.rem(self.region, 2)
        self.beside = (line * 2 + 1 - near, self.shard)
        self.before, self.behind = [(lax.rem(line + d, 4) * 2 + near, self.shard) for d in (1, 3)]
        self.neighbours = [self.sibling, self.across, self.above, self.below, self.beside, self.before, self.behind]

    def at(self, side, z):
        return side * 4 + z

    def device(self, chip, core=None):
        return (self.region, chip * 2 + (self.core if core is None else core))

    def greet(self):
        barrier = pltpu.get_barrier_semaphore()
        for device in self.neighbours:
            pl.semaphore_signal(barrier, inc=1, device_id=device, device_id_type=MESH)
        pl.semaphore_wait(barrier, len(self.neighbours))

    def greet_regions(self, seen):
        for device in (self.before, self.behind):
            pl.semaphore_signal(seen.at[0], inc=1, device_id=device, device_id_type=MESH)
        pl.semaphore_wait(seen.at[0], 2)
        pl.semaphore_signal(seen.at[1], inc=1, device_id=self.beside, device_id_type=MESH)
        pl.semaphore_wait(seen.at[1], 1)


class Links:
    def __init__(self, send, recv):
        self.send, self.recv, self.count, self.names = send, recv, 0, {}

    def made(self, name):
        n, make = self.names[name]
        source, target, device = make()
        return pltpu.make_async_remote_copy(
            src_ref=source, dst_ref=target, send_sem=self.send.at[n], recv_sem=self.recv.at[n],
            device_id=device, device_id_type=MESH,
        )

    def go(self, name, make):
        self.names[name] = self.count, make
        self.count += 1
        self.made(name).start()

    def got(self, name):
        self.made(name).wait_recv()

    def settle(self, chosen=lambda name: True):
        for name in [name for name in self.names if chosen(name)]:
            self.made(name).wait_send()
            del self.names[name]


def gather_round(step, layer, links, place, own, panel):
    p_, half = place, ROWS // 2
    here, there = p_.side, p_.other

    def rows(side, z, part, cut=None):
        def give():
            start = p_.device(p_.at(side, z))[1] * ROWS
            if cut is None:
                return panel.at[part, pl.ds(pl.multiple_of(start, ROWS), ROWS), :]
            return panel.at[part, pl.ds(pl.multiple_of(start + cut * half, half), half), :]

        return give

    def go(name, part, piece, device, source=None):
        links.go((layer, part, name), lambda: ((source or piece)(), piece(), device))

    def got(name, part, piece):
        links.got((layer, part, name))
        go("s" + name, part, piece, p_.sibling)

    if step == 0:
        for part in (0, 1):
            mine, source = rows(here, p_.z, part), functools.partial(lambda part: own.at[layer, part], part)
            go("m", part, mine, p_.above, source)
            go("p", part, mine, p_.below, source)
            go("x", part, mine, p_.across, source)
            go("s", part, mine, p_.sibling, source)
    if step == 1:
        for name, z, ahead, cut in (("m", p_.down, p_.above, 0), ("p", p_.up, p_.below, 1)):
            for part in (0, 1):
                got(name, part, rows(here, z, part))
                go("h" + name, part, rows(here, z, part, cut), ahead)
            go("x" + name, 1, rows(here, z, 1), p_.across)
        for part in (0, 1):
            got("x", part, rows(there, p_.z, part))
        go("xm", 0, rows(there, p_.z, 0), p_.above)
        go("xp", 0, rows(there, p_.z, 0), p_.below)
    if step == 2:
        for name, cut in (("hm", 0), ("hp", 1)):
            for part in (0, 1):
                got(name, part, rows(here, p_.far, part, cut))
            go("x" + name, 1, rows(here, p_.far, 1, cut), p_.across)
        for name, z, ahead, cut in (("m", p_.down, p_.above, 0), ("p", p_.up, p_.below, 1)):
            for part in (0, 1):
                got("x" + name, part, rows(there, z, part))
            go("xh" + name, 0, rows(there, z, 0, cut), ahead)
    if step == 3:
        for name, cut in (("xhm", 0), ("xhp", 1)):
            for part in (0, 1):
                got(name, part, rows(there, p_.far, part, cut))
    if step == 4:
        for part in (0, 1):
            for name in ("", "m", "p", "x", "hm", "hp", "xm", "xp", "xhm", "xhp"):
                links.got((layer, part, "s" + name))


GATHER_COPIES = 2 * 4 + 2 * 9 + 4 + 2 + 2 + 2 + 2


def block_order(place):
    return [(1 - n, z) for z in (place.far, place.up, place.down, place.z) for n in (0, 1)]


def sum_step(step, layer, links, place, bufs, block, out, keep):
    p_, half = place, ROWS // 2
    here, there = p_.side, p_.other
    sides = (here, there)
    stage, acc, halves, fulls, cross, halves_b, fulls_b, cross_b = bufs
    top, low = pl.ds(0, half), pl.ds(half, half)
    ways = ((0, p_.up, top, p_.above), (1, p_.down, low, p_.below))

    def go(name, make, *given):
        links.go(("sum", layer, name), functools.partial(make, *given))

    def got(name):
        links.got(("sum", layer, name))

    if step == "to sibling":
        for n, (side, z) in enumerate(block_order(p_)):
            block(p_.at(sides[side], z), p_.rest, lambda part, rows, x, n=n: stage.__setitem__((n, part, rows), x))
            go(("s", n), lambda n: (stage.at[n], acc.at[n], p_.sibling), n)
    if step == "first hop":
        for n, (side, z) in enumerate(block_order(p_)):

            def add(part, rows, x, n=n):
                acc[n, part, rows] = acc[n, part, rows] + x

            got(("s", n))
            block(p_.at(sides[side], z), p_.core, add)
            if n < 2:
                go(("h", 0, side), lambda n, side: (acc.at[n, 0, top], halves.at[0, side], p_.above), n, side)
                go(("h", 1, side), lambda n, side: (acc.at[n, 0, low], halves.at[1, side], p_.below), n, side)
            if side == 1:
                go(("x", n // 2), lambda n: (acc.at[n, 1], cross_b.at[n // 2], p_.across), n)
    if step == "real along z":
        for side in (1, 0):
            for way, _, cut, ahead in ways:
                n = 2 + 2 * way + (1 - side)
                got(("h", way, side))
                acc[n, 0, cut] = acc[n, 0, cut] + halves[way, side]
                go(("f", way, side), lambda n, way, side, ahead: (acc.at[n, 0], fulls.at[way, side], ahead), n, way, side, ahead)
    if step == "imaginary far":
        got(("x", 0))
        acc[1, 1] = acc[1, 1] + cross_b[0]
        for way, _, cut, ahead in ways:
            go(("hb", way), lambda way, cut, ahead: (acc.at[1, 1, cut], halves_b.at[way], ahead), way, cut, ahead)
    if step == "real across":
        for way in (0, 1):
            got(("f", way, 1))
        acc[6, 0] = acc[6, 0] + fulls[0, 1] + fulls[1, 1]
        go("c", lambda: (acc.at[6, 0], cross, p_.across))
    if step == "imaginary along z":
        for way, _, cut, ahead in ways:
            n = 3 + 2 * way
            got(("x", 1 + way))
            acc[n, 1] = acc[n, 1] + cross_b[1 + way]
            got(("hb", way))
            acc[n, 1, cut] = acc[n, 1, cut] + halves_b[way]
            go(("fb", way), lambda n, way, ahead: (acc.at[n, 1], fulls_b.at[way], ahead), n, way, ahead)
    if step == "last":
        got(("x", 3))
        for way in (0, 1):
            got(("f", way, 0))
        acc[7, 0] = acc[7, 0] + fulls[0, 0] + fulls[1, 0]
        acc[7, 1] = acc[7, 1] + cross_b[3]
        for way in (0, 1):
            got(("fb", way))
        out[layer, 1] = acc[7, 1] + fulls_b[0] + fulls_b[1]
        got("c")
        out[layer, 0] = acc[7, 0] + cross[...]
        keep(layer)


SUM_COPIES = 8 + 4 + 4 + 4 + 2 + 1 + 2
SUM_BUFFERS = [
    pltpu.VMEM((CHIPS, 2, ROWS, COLS), f32),
    pltpu.VMEM((CHIPS, 2, ROWS, COLS), f32),
    pltpu.VMEM((2, 2, ROWS // 2, COLS), f32),
    pltpu.VMEM((2, 2, ROWS, COLS), f32),
    pltpu.VMEM((ROWS, COLS), f32),
    pltpu.VMEM((2, ROWS // 2, COLS), f32),
    pltpu.VMEM((2, ROWS, COLS), f32),
    pltpu.VMEM((4, ROWS, COLS), f32),
]


def probe_round(step, links, place, part, bufs, out):
    p_ = place
    acc, mine, all_regions = bufs

    def go(name, make, *given):
        links.go(("probe", name), functools.partial(make, *given))

    def got(name):
        links.got(("probe", name))

    def rows(shard):
        return pl.ds(pl.multiple_of(shard * PROBE_ROWS, PROBE_ROWS), PROBE_ROWS)

    if step == 0:
        for chip in range(CHIPS):
            go(("s", chip), lambda chip: (part.at[:, rows(chip * 2 + 1 - p_.core), :], acc.at[chip], p_.sibling), chip)
    if step == 1:
        for chip in range(CHIPS):
            got(("s", chip))
            acc[chip] = acc[chip] + part[:, rows(chip * 2 + p_.core), :]
        for d in range(1, CHIPS):
            chip = lax.rem(p_.chip + d, CHIPS)
            go(("r", d), lambda chip, d: (acc.at[chip], mine.at[d], p_.device(chip)), chip, d)
    if step == 2:
        total = acc[p_.chip]
        for d in range(1, CHIPS):
            got(("r", d))
            total = total + mine[d]
        all_regions[p_.region] = total
        for d in range(1, REGIONS):
            there = lax.rem(p_.region + d, REGIONS)
            go(("g", d), lambda there: (all_regions.at[p_.region], all_regions.at[p_.region], (there, p_.shard)), there)
    if step == 3:
        for d in range(1, REGIONS):
            got(("g", d))
        total = all_regions[0]
        for region in range(1, REGIONS):
            total = total + all_regions[region]
        out[:, rows(p_.shard), :] = total * (REGIONS * SHARDS) ** -0.5
        for d in range(1, SHARDS):
            there = lax.rem(p_.shard + d, SHARDS)
            go(("b", d), lambda there: (out.at[:, rows(p_.shard), :], out.at[:, rows(p_.shard), :], (p_.region, there)), there)
    if step == 4:
        for d in range(1, SHARDS):
            got(("b", d))


PROBE_COPIES = 8 + 7 + 7 + 15
PROBE_BUFFERS = [
    pltpu.VMEM((CHIPS, 2, PROBE_ROWS, SIDE), f32),
    pltpu.VMEM((CHIPS, 2, PROBE_ROWS, SIDE), f32),
    pltpu.VMEM((REGIONS, 2, PROBE_ROWS, SIDE), f32),
]


def kernel(corners, counts, own, probe_in, measured_in, tab_in, tab_t_in, kern_in, mix_in, out_to, probe_to, *scratch):
    panels, scratch = scratch[:LAYERS], scratch[LAYERS:]
    sums, scratch = [scratch[8 * n : 8 * n + 8] for n in range(LAYERS)], scratch[8 * LAYERS :]
    probe_bufs, scratch = scratch[:3], scratch[3:]
    probe, measured, tab, tab_t, kern, mix, out, probe_out, scratch = *scratch[:8], scratch[8:]
    window, psi, chi, target, placed, probe_sum, send_sem, recv_sem, load_sem, keep_sem, seen = scratch
    place = Place()
    links = Links(send_sem, recv_sem)
    loads = [
        pltpu.make_async_copy(source, into, load_sem.at[n])
        for n, (source, into) in enumerate(
            ((probe_in, probe), (mix_in, mix), (measured_in, measured), (tab_in, tab), (tab_t_in, tab_t), (kern_in, kern))
        )
    ]
    loads += [
        pltpu.make_async_copy(
            own.at[layer], panels[layer].at[:, pl.ds(pl.multiple_of(place.shard * ROWS, ROWS), ROWS), :], load_sem.at[6 + layer]
        )
        for layer in range(LAYERS)
    ]
    for load in loads:
        load.start()
    place.greet()

    def kept(layer):
        return pltpu.make_async_copy(out.at[layer], out_to.at[layer], keep_sem.at[layer])

    def gather(layer, step):
        gather_round(step, layer, links, place, own, panels[layer])

    def collect(layer, step):
        sum_step(step, layer, links, place, sums[layer], block, out, lambda layer: kept(layer).start())

    def collect_probe(step):
        probe_round(step, links, place, probe_sum, probe_bufs, probe_out)

    def scans(body, between=()):
        def step(scan, carry):
            body(scan)
            for n, act in enumerate(between):
                pl.when(scan == n)(act)
            return carry

        lax.fori_loop(0, SCANS, step, 0)

    def corner(scan):
        row = jnp.minimum(jnp.maximum(corners[0, scan, 0] - place.region * BAND, 0), BAND - SIDE)
        return row, jnp.minimum(jnp.maximum(corners[0, scan, 1], 0), COLS - SIDE)

    def fetch(scan, layer):
        row, column = corner(scan)
        index = lax.broadcasted_iota(jnp.int32, (SIDE, SIDE), 0)
        in_left = lax.broadcasted_iota(jnp.int32, (SIDE, SIDE), 1) >= column
        for part in (0, 1):
            found = None
            for first in range(BAND - SIDE, -1, -SIDE):
                rows = slice(first, first + SIDE)
                piece = jnp.where(in_left, panels[layer][part, rows, :SIDE], panels[layer][part, rows, SIDE:])
                found = piece if found is None else jnp.where(index >= row - first, piece, found)
            window[scan, layer, part] = found

    def turned(x, scan, back):
        row, column = corner(scan)
        a = lax.broadcasted_iota(jnp.int32, (SIDE, SIDE), 0)
        b = lax.broadcasted_iota(jnp.int32, (SIDE, SIDE), 1)
        down, along = (b - a - row, a - b - column) if back else (a - b - row, b - a - column)
        down, along = [
            jnp.where(jnp.bitwise_and(far, SIDE - 1) == 0, 1.0, 0.0).astype(bf16) for far in (down, along)
        ]
        high, low = split(x)
        high, low = split(dot(high, along) + dot(low, along))
        return dot(down, high) + dot(down, low)

    def block(chip, core, store):
        first = (chip * 2 + core) * ROWS

        def some(step, carry):
            at = step * 16
            source = pl.ds(pl.multiple_of(lax.rem(first, SIDE) + at, 16), 16)
            rows = lax.broadcasted_iota(jnp.int32, (16, SIDE), 0) + first + at
            columns = lax.broadcasted_iota(jnp.int32, (16, SIDE), 1)
            total = [[0.0, 0.0], [0.0, 0.0]]
            for scan in range(SCANS):
                row, column = corner(scan)
                inside = jnp.logical_and(rows >= row, rows < row + SIDE)
                left = jnp.logical_and(inside, columns >= column)
                right = jnp.logical_and(inside, columns < column)
                for part in (0, 1):
                    piece = placed[scan, part, source, :]
                    for n, mask in enumerate((left, right)):
                        total[part][n] = total[part][n] + jnp.where(mask, piece, 0.0)
            for part in (0, 1):
                store(part, pl.ds(pl.multiple_of(at, 16), 16), cat(total[part], 1))
            return carry

        lax.fori_loop(0, ROWS // 16, some, 0)

    def reorder(scan):
        rows = None
        for piece in split(measured[0, scan]):
            rows = dot(piece, mix[0]) + (0 if rows is None else rows)
        both = None
        for piece in split(rows):
            both = dot(mix[1], piece) + (0 if both is None else both)
        target[scan] = both

    def illuminate(scan):
        for part in (0, 1):
            psi[scan, 0, part] = turned(probe[part], scan, False)

    def wave(scan, layer):
        return psi[scan, layer, 0], psi[scan, layer, 1]

    def enter(scan, layer):
        fetch(scan, layer)
        return multiply(*wave(scan, layer), window[scan, layer, 0], window[scan, layer, 1])

    def go_on(layer):
        def body(scan):
            re, im = propagate(*enter(scan, layer), tab, tab_t, kern, False)
            psi[scan, layer + 1, 0], psi[scan, layer + 1, 1] = re, im

        return body

    def leave(scan, layer, re, im):
        placed[scan, 0], placed[scan, 1] = conj_multiply(*wave(scan, layer), re, im)
        re, im = conj_multiply(window[scan, layer, 0], window[scan, layer, 1], re, im)
        if layer > 0:
            chi[scan, 0], chi[scan, 1] = re, im
        else:
            probe_sum[0] = probe_sum[0] + turned(re, scan, True)
            probe_sum[1] = probe_sum[1] + turned(im, scan, True)

    def turn(scan):
        parts = []
        for at, y in zip((0, HALF), forward(*enter(scan, LAYERS - 1), tab, tab_t)):
            re, im = y[:HALF], y[HALF:]
            residual = (re * re + im * im - target[scan, at : at + HALF, :]) * jnp.where(scan < counts[0], 1.0, 0.0)
            parts.append(cat([residual * re, residual * im], 0))
        leave(scan, LAYERS - 1, *inverse(*parts, tab, tab_t))

    def go_back(layer):
        def body(scan):
            leave(scan, layer, *propagate(chi[scan, 0], chi[scan, 1], tab, tab_t, kern, True))

        return body

    def then(*acts):
        def run():
            for act, layer, step in acts:
                act(layer, step)

        return run

    def prepare(scan):
        reorder(scan)
        illuminate(scan)

    gather(0, 0)
    gather(1, 0)
    gather(2, 0)
    probe_sum[...] = jnp.zeros_like(probe_sum)
    for load in loads:
        load.wait()
    scans(prepare)
    gather(0, 1)
    gather(1, 1)
    place.greet_regions(seen)
    gather(2, 1)
    gather(0, 2)
    gather(1, 2)
    gather(0, 3)
    gather(2, 2)
    gather(0, 4)
    scans(
        go_on(0),
        [
            then((gather, 1, 3)),
            then((gather, 2, 3)),
        ],
    )
    gather(1, 4)
    scans(go_on(1))
    gather(2, 4)
    scans(turn)
    collect(2, "to sibling")
    collect(2, "first hop")
    scans(
        go_back(1),
        [
            then(),
            then((collect, 2, "real along z")),
            then((collect, 2, "imaginary far")),
        ],
    )
    collect(1, "to sibling")
    collect(1, "first hop")
    scans(
        go_back(0),
        [
            then((collect, 2, "imaginary along z")),
            then((collect, 2, "real across")),
            then((collect, 1, "real along z")),
            then((collect, 1, "imaginary far")),
        ],
    )
    collect_probe(0)
    collect(0, "to sibling")
    collect(0, "first hop")
    collect_probe(1)
    collect(2, "last")
    collect(1, "imaginary along z")
    collect_probe(2)
    collect(1, "real across")
    collect(0, "real along z")
    collect_probe(3)
    collect(0, "imaginary far")
    collect(1, "last")
    collect(0, "real across")
    collect(0, "imaginary along z")
    collect_probe(4)
    probe_kept = pltpu.make_async_copy(probe_out, probe_to, keep_sem.at[LAYERS])
    probe_kept.start()
    collect(0, "last")
    for layer in range(LAYERS):
        kept(layer).wait()
    probe_kept.wait()
    links.settle()


def body(object_slices, probe_field, positions, scan_counts, measured):
    tab, tab_t = transform_tables()
    hbm, smem = pl.BlockSpec(memory_space=pl.ANY), pl.BlockSpec(memory_space=pltpu.SMEM)
    copies = LAYERS * (GATHER_COPIES + SUM_COPIES) + PROBE_COPIES
    field = (SIDE, SIDE)
    return pl.pallas_call(
        kernel,
        out_shape=(
            jax.ShapeDtypeStruct((LAYERS, 2, ROWS, COLS), f32),
            jax.ShapeDtypeStruct((2, *field), f32),
        ),
        in_specs=[smem, smem] + [hbm] * 7,
        out_specs=(hbm, hbm),
        scratch_shapes=[pltpu.VMEM((2, BAND, COLS), f32)] * LAYERS
        + SUM_BUFFERS * LAYERS
        + PROBE_BUFFERS
        + [
            pltpu.VMEM((2, *field), f32),
            pltpu.VMEM((1, SCANS, *field), f32),
            pltpu.VMEM(tab.shape, bf16),
            pltpu.VMEM(tab.shape, bf16),
            pltpu.VMEM((2, *field), f32),
            pltpu.VMEM((2, *field), bf16),
            pltpu.VMEM((LAYERS, 2, ROWS, COLS), f32),
            pltpu.VMEM((2, *field), f32),
            pltpu.VMEM((SCANS, LAYERS, 2, *field), f32),
            pltpu.VMEM((SCANS, LAYERS, 2, *field), f32),
            pltpu.VMEM((SCANS, 2, *field), f32),
            pltpu.VMEM((SCANS, *field), f32),
            pltpu.VMEM((SCANS, 2, *field), f32),
            pltpu.VMEM((2, *field), f32),
            pltpu.SemaphoreType.DMA((copies,)),
            pltpu.SemaphoreType.DMA((copies,)),
            pltpu.SemaphoreType.DMA((6 + LAYERS,)),
            pltpu.SemaphoreType.DMA((LAYERS + 1,)),
            pltpu.SemaphoreType.REGULAR((2,)),
        ],
        compiler_params=pltpu.CompilerParams(collective_id=0, has_side_effects=True, vmem_limit_bytes=60 * 2**20),
    )(positions, scan_counts, object_slices, probe_field, measured, tab, tab_t, propagator(), shuffles())


def solution(mesh):
    return jax.shard_map(
        body,
        mesh=mesh,
        in_specs=(
            P(None, None, ("region", "shard"), None),
            P(),
            P(("region", "shard"), None, None),
            P(("region", "shard")),
            P(("region", "shard"), None, None, None),
        ),
        out_specs=(P(None, None, ("region", "shard"), None), P()),
        check_vma=False,
    )
```
